256 devices in a mesh: expert: 16 (over z, core), panel: 16 (over x, y).
Axes of the slice: x: 4, y: 4, z: 8, core: 2. Of those that a mesh axis runs over, the one named last changes fastest.
Arguments:
- queries: bfloat16 [2048, 4, 7168], P('expert', None, 'panel'), may hold values from -6 to 6
- expert_ids: int32 [2048, 4], P('expert'), may hold values from 0 to 15, all different within a row; in each aligned block of 128 rows (0 to 127, 128 to 255, ...) at most 64 rows name the same one
- mix_weights: float32 [2048, 4], P('expert'), may hold values from 0.2 to 1
- factors: bfloat16 [16, 7168, 7168], P('expert', 'panel'), as said below
Outputs:
- combined: bfloat16 [2048, 7168], P('expert', 'panel')
The draws below stay inside these ranges and needn't reach their ends.
Inputs may be any that keep to these rules, and one draw needn't show every extreme that they name: `expert_ids`: each token names 4 different experts; the 128 tokens held at one position along `expert` send at most 64 rows to any one expert, and some expert receives exactly 64 of them. `factors`: each expert's factor is symmetric.
All inputs are finite; a program needn't handle non-finite values.
Results may differ from the reference program's by a relative error of at most 0.005.
Values may be sent and summed in bfloat16 or wider, within the bound.
No kernel may reach another device: no remote copies, remote signals or barrier semaphores. Data moves between devices by JAX's collectives and lax.ppermute only.
A program may use at most 192 MiB of HBM per device.

```python
import math
import jax
import jax.numpy as jnp
import numpy as np
from jax import lax

D = 7168
TOPK = 4
TOK_DEV = 128
EXPERTS = 16
TOKENS = 2048
CAP = 64
N_EXPERT = 16


def draw_factors(key, part):
    key = jax.random.fold_in(key, 7)

    def draw_expert(subkey):
        key_off, key_diag = jax.random.split(subkey)
        entries = jax.random.normal(key_off, (D, D), jnp.float32)
        symmetric = (entries + entries.T) * (0.25 / math.sqrt(2.0 * D))
        diagonal = jnp.exp(jax.random.uniform(key_diag, (D,), jnp.float32, 0.0, math.log(2.5)))
        return (symmetric + jnp.diag(diagonal)).astype(jnp.bfloat16)
    expert_keys = jax.random.split(key, EXPERTS)
    return lax.map(draw_expert, expert_keys)


def levels(own_key, dims, cuts, low, largest):
    def one(axis_at, parts):
        steps = jax.random.uniform(jax.random.fold_in(jax.random.fold_in(own_key, 6), axis_at), (parts,), jnp.float32, low / len(cuts), largest / len(cuts))
        return jnp.repeat(jnp.exp(steps), dims[axis_at] // parts).reshape((-1,) + (1,) * (len(dims) - axis_at - 1))

    factor_of = one(*cuts[0])
    for cut in cuts[1:]:
        factor_of = factor_of * one(*cut)
    return factor_of


def deal_out(own_key, own, number, rows, amount, top, bound, lean):
    ranking = jax.random.permutation(own_key, amount)
    packed, common = portions_of(amount, rows * top, bound, lean, True), portions_of(amount, rows * top, bound, lean, False)
    places = jnp.arange(amount)

    def named(tallies, offset_by):
        used = int((tallies > 0).sum())
        fixed = max(1, used // 4)
        moved = fixed + (places - fixed + offset_by * (used - fixed)) % max(1, amount - fixed)
        return jnp.zeros((amount,), jnp.int32).at[ranking[jnp.where(places < fixed, places, moved)]].set(jnp.asarray(tallies, jnp.int32))

    tallies = jnp.where(number % 4 == 0, named(packed, number // 4), named(common, number - number // 4 - 1))
    mixed = jax.random.permutation(jax.random.fold_in(own, 3), amount)
    source_of, taker = mixed[0:amount // 2 * 2:2], mixed[1:amount // 2 * 2:2]
    room = jnp.minimum(tallies[source_of] - 1, bound - tallies[taker]) // 2
    room = jnp.where((source_of == ranking[0]) | (taker == ranking[0]) | (tallies[taker] == 0), 0, jnp.maximum(room, 0))
    moved = jax.random.randint(jax.random.fold_in(own, 4), (amount // 2,), 0, 1 << 20) % (room + 1)
    tallies = tallies.at[source_of].add(-moved).at[taker].add(moved)
    labels = jnp.searchsorted(jnp.cumsum(tallies), jnp.arange(rows * top), side="right").astype(jnp.int32)
    listing = labels.reshape(top, rows).T
    listing = listing[jax.random.permutation(jax.random.fold_in(own, 1), rows)]
    offset_by = jax.random.randint(jax.random.fold_in(own, 2), (rows, 1), 0, top)
    return jnp.take_along_axis(listing, (jnp.arange(top)[None, :] + offset_by) % top, axis=1)


def portions_of(count, total, reach, lean, full):
    loads = [(1 << 20) // math.isqrt(grade ** lean) + 1 for grade in range(1, count + 1)]
    largest = reach if full else min(reach, max(-(-total // count), total * loads[0] // sum(loads)))
    least = 1 if total - largest >= count - 1 else 0
    counts, surplus = [largest] + [least] * (count - 1), total - largest - least * (count - 1)
    while surplus > 0:
        free = [i for i in range(1, count) if counts[i] < largest] or [i for i in range(1, count) if counts[i] < reach]
        whole, remaining = sum([loads[i] for i in free]), surplus
        for i in free:
            more = min(reach - counts[i], max(1, remaining * loads[i] // whole), surplus)
            counts[i] = counts[i] + more
            surplus = surplus - more
    return np.array(counts)


def gaussian(key, shape, spread, reach, cuts=(), kind=jnp.bfloat16):
    factor_of = levels(key, shape, cuts, -0.22, 0.18) if cuts else 1.0
    drawn = jax.random.normal(key, shape, jnp.float32) * spread * factor_of
    return jnp.minimum(jnp.maximum(drawn, -reach), reach).astype(kind)


def setup_inputs(seed: int = 0) -> dict:
    arg_keys = jax.random.split(jax.random.key(seed), 5)
    queries = gaussian(arg_keys[0], (TOKENS, TOPK, D), 1.0, 6.0, ((0, 16), (2, 16)))
    expert_ids_keys = jax.random.split(jax.random.fold_in(arg_keys[1], 1), TOKENS // TOK_DEV)
    expert_ids_turns = jax.random.permutation(jax.random.fold_in(arg_keys[1], 3), TOKENS // TOK_DEV)
    expert_ids = jax.vmap(lambda own, number: deal_out(jax.random.fold_in(arg_keys[1], 2), own, number, TOK_DEV, EXPERTS, TOPK, CAP, 2))(expert_ids_keys, expert_ids_turns).reshape((TOKENS, TOPK))
    mix_weights = jnp.clip(0.2 + 0.8 * jax.random.uniform(arg_keys[2], (TOKENS, TOPK), jnp.float32) ** levels(arg_keys[2], (TOKENS, TOPK), ((0, 16),), -0.2, 0.2), 0.2, 1.0)
    factors = draw_factors(jax.random.fold_in(arg_keys[4], 71), 0)
    return dict(queries=queries, expert_ids=expert_ids, mix_weights=mix_weights, factors=factors)


def reference(queries, expert_ids, mix_weights, factors):
    capacity = 2 * TOK_DEV * TOPK // N_EXPERT
    src_rows = TOK_DEV * TOPK
    flat_ids = expert_ids.reshape(N_EXPERT, src_rows).astype(jnp.int32)
    onehot = (flat_ids[:, :, None] == jnp.arange(EXPERTS, dtype=jnp.int32)[None, None, :]).astype(jnp.int32)
    position = (jnp.sum(jnp.cumsum(onehot, axis=1) * onehot, axis=2) - 1).astype(jnp.int32)
    source_idx = jnp.broadcast_to(jnp.arange(N_EXPERT, dtype=jnp.int32)[:, None], (N_EXPERT, src_rows))
    flat_q = queries.reshape(N_EXPERT, src_rows, D)
    buffers = jnp.zeros((EXPERTS, N_EXPERT, capacity, D), queries.dtype)
    buffers = buffers.at[flat_ids, source_idx, position].set(flat_q)

    def apply_one(operands):
        rows_in, factor = operands
        product = jnp.dot(rows_in.reshape(N_EXPERT * capacity, D), factor, preferred_element_type=jnp.float32)
        return product.astype(jnp.bfloat16)

    precond = lax.map(apply_one, (buffers, factors))
    precond = precond.reshape(EXPERTS, N_EXPERT, capacity, D)
    returned = precond[flat_ids, source_idx, position]
    returned = returned.reshape(TOKENS, TOPK, D).astype(jnp.float32)
    combined = jnp.sum(returned * mix_weights.astype(jnp.float32)[:, :, None], axis=1)
    return combined.astype(jnp.bfloat16)
```

```python
import functools

import jax
import jax.numpy as jnp
from jax import lax
from jax.experimental import pallas as pl
from jax.experimental.pallas import tpu as pltpu
from jax.sharding import PartitionSpec as P

SIDE = 4
CHIPS = 8
SLOTS = 64
WIDE = 2 * SLOTS
X_FIRST = (2, 6, 3, 5)
Y_FIRST = (0, 1, 7, 4)
WINDOW = 512
STEPS = (0, -1, 1, 2)
VMEM = 50 * 1024 * 1024


def along_x(by):
    return [(x * SIDE + y, (x + by) % SIDE * SIDE + y) for x in range(SIDE) for y in range(SIDE)]


def along_y(by):
    return [(x * SIDE + y, x * SIDE + (y + by) % SIDE) for x in range(SIDE) for y in range(SIDE)]


def along_z(by):
    return [(z * 2 + c, (z + by) % CHIPS * 2 + c) for z in range(CHIPS) for c in range(2)]


SWAP = [(i, i ^ 1) for i in range(2 * CHIPS)]


def dot(a, b, dims=((1,), (0,))):
    return lax.dot_general(a, b, (dims, ((), ())), preferred_element_type=jnp.float32)


def route_kernel(own_ids, own_mix, own_rows, other_ids, other_mix, other_rows, *rest):
    blocks, (high, low), (turned, chosen) = rest[:CHIPS], rest[CHIPS : CHIPS + 2], rest[CHIPS + 2 :]
    me = lax.axis_index("expert")
    z, core = me // 2, me % 2
    top_count, tokens, _ = own_rows.shape
    width = CHIPS * WIDE
    lane = lax.broadcasted_iota(jnp.int32, (tokens, width), 1)
    earlier = (
        lax.broadcasted_iota(jnp.int32, (tokens, tokens), 0)
        > lax.broadcasted_iota(jnp.int32, (tokens, tokens), 1)
    ).astype(jnp.bfloat16)
    experts = lax.broadcasted_iota(jnp.int32, (tokens, 2 * CHIPS), 1)
    sides = (own_ids, own_mix, own_rows), (other_ids, other_mix, other_rows)
    for n, (ids, mix, rows) in enumerate(sides):
        source = core if n == 0 else 1 - core
        ids, mix = ids[...].T, mix[...].T
        named = [ids[:, j : j + 1] for j in range(top_count)]
        hits = [(experts == one).astype(jnp.float32) for one in named]
        before = dot(earlier, sum(hits).astype(jnp.bfloat16))
        weights = jnp.zeros((tokens, width), jnp.float32)
        for j in range(top_count):
            slot = jnp.sum(hits[j] * before, axis=1, keepdims=True).astype(jnp.int32)
            shift = ((named[j] >> 1) - z + CHIPS) & (CHIPS - 1)
            place = jnp.where((named[j] & 1) == core, shift * WIDE + source * SLOTS + slot, -1)
            taken = lane == place
            span = pl.ds((n * top_count + j) * tokens, tokens)
            chosen[span, :] = taken.astype(jnp.float32).astype(jnp.bfloat16)
            turned[:, span] = rows[j].T
            weights = jnp.where(taken, mix[:, j : j + 1], weights)
        upper = weights.astype(jnp.bfloat16)
        high[pl.ds(n * tokens, tokens), :] = upper
        low[pl.ds(n * tokens, tokens), :] = (weights - upper.astype(jnp.float32)).astype(jnp.bfloat16)
    for k in range(0, CHIPS, 2):
        pair = dot(turned[...], chosen[:, k * WIDE : (k + 2) * WIDE]).astype(jnp.bfloat16)
        blocks[k][...] = pair[:, :WIDE]
        blocks[k + 1][...] = pair[:, WIDE:]


def route(own, other):
    top_count, tokens, feat = own[2].shape
    width = CHIPS * WIDE
    outs = [jax.ShapeDtypeStruct((feat, WIDE), jnp.bfloat16)] * CHIPS
    outs += [jax.ShapeDtypeStruct((2 * tokens, width), jnp.bfloat16)] * 2
    got = pl.pallas_call(
        route_kernel,
        out_shape=outs,
        scratch_shapes=[
            pltpu.VMEM((feat, 2 * top_count * tokens), jnp.bfloat16),
            pltpu.VMEM((2 * top_count * tokens, width), jnp.bfloat16),
        ],
        compiler_params=pltpu.CompilerParams(vmem_limit_bytes=VMEM),
        name="route",
    )(*own, *other)
    return got[:CHIPS], got[CHIPS], got[CHIPS + 1]


def ring_kernel(x_first, early, factor, *rest):
    sources, rest = rest[: 3 if early else 2], rest[3 if early else 2 :]
    before, outs, (held, gathered, sems) = rest[:-3][: 1 - early], rest[1 - early : -3], rest[-3:]
    panel = lax.axis_index("panel")
    x, y = panel // SIDE, panel % SIDE
    feat, half = held.shape[1], held.shape[1] // 2
    width = gathered.shape[2]
    copies = []
    for g, second in enumerate(range(SIDE - 1) if early else (SIDE - 1,)):
        for first in range(SIDE):
            dx, dy = (STEPS[first], STEPS[second]) if x_first else (STEPS[second], STEPS[first])
            owner = (x + dx + SIDE) % SIDE * SIDE + (y + dy + SIDE) % SIDE
            lead = owner % 2 * (WINDOW - feat)
            top = first * WINDOW
            gathered[g, pl.ds(top, WINDOW - feat), :] = jnp.zeros((WINDOW - feat, width), gathered.dtype)
            gathered[g, pl.ds(top + feat, WINDOW - feat), :] = jnp.zeros((WINDOW - feat, width), gathered.dtype)
            columns = pl.ds(pl.multiple_of(owner * feat - lead, 128), WINDOW)
            window = held.at[g, :, pl.ds(top, WINDOW)]
            copies.append(pltpu.make_async_copy(factor.at[:, columns], window, sems.at[len(copies)]))
            copies[-1].start()
            for j in range(2):
                source = sources[second].at[j, first] if early else sources[j].at[first]
                target = gathered.at[g, pl.ds(pl.multiple_of(top + j * half + lead, 16), half)]
                copies.append(pltpu.make_async_copy(source, target, sems.at[len(copies)]))
                copies[-1].start()
    count = len(copies) // held.shape[0]
    for g in range(held.shape[0]):
        for copy in copies[g * count : (g + 1) * count]:
            copy.wait()
        total = dot(held[g], gathered[g])
        if early:
            outs[0][...] = total if g == 0 else total + outs[0][...]
    if not early:
        total = (total + before[0][...]).astype(jnp.bfloat16)
        for b, block in enumerate(outs):
            block[...] = total[:, b * WIDE : (b + 1) * WIDE]


def times_ring(factor, x_first, pieces, before=()):
    feat, full = factor.shape
    width = pieces[0].shape[-1]
    early = not before
    groups = SIDE - 1 if early else 1
    anywhere, vmem = pl.BlockSpec(memory_space=pl.ANY), pl.BlockSpec(memory_space=pltpu.VMEM)
    if early:
        outs = [jax.ShapeDtypeStruct((feat, width), jnp.float32)]
    else:
        outs = [jax.ShapeDtypeStruct((feat, WIDE), jnp.bfloat16)] * (width // WIDE)
    depth = SIDE * WINDOW
    return pl.pallas_call(
        functools.partial(ring_kernel, x_first, early),
        in_specs=[anywhere] * (1 + len(pieces)) + [vmem] * len(before),
        out_specs=[vmem] * len(outs),
        out_shape=outs,
        scratch_shapes=[
            pltpu.VMEM((groups, feat, depth), jnp.bfloat16),
            pltpu.VMEM((groups, depth, width), jnp.bfloat16),
            pltpu.SemaphoreType.DMA((groups * SIDE * 3,)),
        ],
        compiler_params=pltpu.CompilerParams(vmem_limit_bytes=VMEM),
        cost_estimate=pl.CostEstimate(
            flops=2 * groups * feat * depth * width,
            bytes_accessed=2 * groups * depth * (feat + width),
            transcendentals=0,
        ),
        name="times_ring_early" if early else "times_ring_late",
    )(factor, *pieces, *before)


def go_round(parts, way):
    behind, ahead = (lax.ppermute(parts, "panel", way(by)) for by in (1, -1))
    return behind, ahead, lax.ppermute(behind[0], "panel", way(1)), lax.ppermute(ahead[1], "panel", way(-1))


def ring_product(factor, block, x_first):
    feat, width = block.shape
    ways = (along_x, along_y) if x_first else (along_y, along_x)
    mine = block.reshape(2, feat // 2, width)
    behind, ahead, *across = go_round(mine, ways[0])
    line = jnp.stack([jnp.stack([mine[j], behind[j], ahead[j], across[j]]) for j in range(2)])
    behind, ahead, *across = go_round(line, ways[1])
    early = times_ring(factor, x_first, [line, behind, ahead])
    return times_ring(factor, x_first, across, early)


def combine_kernel(count, high, low, *rest):
    returned, (own, other) = rest[:count], rest[count:]
    tokens = own.shape[0]
    total = None
    for k, block in enumerate(returned):
        span = pl.ds(k * WIDE, WIDE)
        for part in (high, low):
            term = dot(part[:, span], block[...], ((1,), (1,)))
            total = term if total is None else total + term
    own[...] = total[:tokens]
    other[...] = total[tokens:]


def combine(high, low, returned):
    feat = returned[0].shape[0]
    return pl.pallas_call(
        functools.partial(combine_kernel, len(returned)),
        out_shape=[jax.ShapeDtypeStruct((high.shape[0] // 2, feat), jnp.float32)] * 2,
        compiler_params=pltpu.CompilerParams(vmem_limit_bytes=VMEM),
        name="combine",
    )(high, low, *returned)


def on_device(queries, expert_ids, mix_weights, factors):
    swap = lambda a: lax.ppermute(a, "expert", SWAP)
    mine = expert_ids.T, mix_weights.T, jnp.transpose(queries, (1, 0, 2))
    blocks, high, low = route(mine, tuple(map(swap, mine)))
    arrived = {k: lax.ppermute(blocks[k], "expert", along_z(k)) if k else blocks[k] for k in range(CHIPS)}

    product = {}
    for shifts in (X_FIRST, Y_FIRST):
        block = jnp.concatenate([arrived[k] for k in shifts], 1)
        product |= dict(zip(shifts, ring_product(factors[0], block, shifts is X_FIRST)))

    returned = [lax.ppermute(product[k], "expert", along_z(-k)) if k else product[k] for k in range(CHIPS)]
    own, other = combine(high, low, returned)
    return (own + swap(other)).astype(jnp.bfloat16)


def solution(mesh):
    in_specs = (
        P("expert", None, "panel"),
        P("expert", None),
        P("expert", None),
        P("expert", "panel", None),
    )
    out_specs = P("expert", "panel")
    return jax.shard_map(
        on_device, mesh=mesh, in_specs=in_specs, out_specs=out_specs, check_vma=False
    )
```

```python
import functools

import jax
import jax.numpy as jnp
from jax import lax
from jax.experimental import pallas as pl
from jax.experimental.pallas import tpu as pltpu
from jax.sharding import PartitionSpec as P

SIDE = 4
CHIPS = 8
SLOTS = 64
WIDE = 2 * SLOTS
X_FIRST = (2, 6, 3, 5)
Y_FIRST = (0, 1, 7, 4)
WINDOW = 512
STEPS = (0, -1, 1, 2)
VMEM = 50 * 1024 * 1024


def along_x(by):
    return [(x * SIDE + y, (x + by) % SIDE * SIDE + y) for x in range(SIDE) for y in range(SIDE)]


def along_y(by):
    return [(x * SIDE + y, x * SIDE + (y + by) % SIDE) for x in range(SIDE) for y in range(SIDE)]


def along_z(by):
    return [(z * 2 + c, (z + by) % CHIPS * 2 + c) for z in range(CHIPS) for c in range(2)]


SWAP = [(i, i ^ 1) for i in range(2 * CHIPS)]


def dot(a, b, dims=((1,), (0,))):
    return lax.dot_general(a, b, (dims, ((), ())), preferred_element_type=jnp.float32)


def route_kernel(own_ids, own_mix, own_rows, other_ids, other_mix, other_rows, *rest):
    blocks, (high, low), (turned, chosen) = rest[:CHIPS], rest[CHIPS : CHIPS + 2], rest[CHIPS + 2 :]
    me = lax.axis_index("expert")
    z, core = me // 2, me % 2
    top_count, tokens, _ = own_rows.shape
    width = CHIPS * WIDE
    lane = lax.broadcasted_iota(jnp.int32, (tokens, width), 1)
    earlier = (
        lax.broadcasted_iota(jnp.int32, (tokens, tokens), 0)
        > lax.broadcasted_iota(jnp.int32, (tokens, tokens), 1)
    ).astype(jnp.bfloat16)
    experts = lax.broadcasted_iota(jnp.int32, (tokens, 2 * CHIPS), 1)
    sides = (own_ids, own_mix, own_rows), (other_ids, other_mix, other_rows)
    for n, (ids, mix, rows) in enumerate(sides):
        source = core if n == 0 else 1 - core
        ids, mix = ids[...].T, mix[...].T
        named = [ids[:, j : j + 1] for j in range(top_count)]
        hits = [(experts == one).astype(jnp.float32) for one in named]
        before = dot(earlier, sum(hits).astype(jnp.bfloat16))
        weights = jnp.zeros((tokens, width), jnp.float32)
        for j in range(top_count):
            slot = jnp.sum(hits[j] * before, axis=1, keepdims=True).astype(jnp.int32)
            shift = ((named[j] >> 1) - z + CHIPS) & (CHIPS - 1)
            place = jnp.where((named[j] & 1) == core, shift * WIDE + source * SLOTS + slot, -1)
            taken = lane == place
            span = pl.ds((n * top_count + j) * tokens, tokens)
            chosen[span, :] = taken.astype(jnp.float32).astype(jnp.bfloat16)
            turned[:, span] = rows[j].T
            weights = jnp.where(taken, mix[:, j : j + 1], weights)
        upper = weights.astype(jnp.bfloat16)
        high[pl.ds(n * tokens, tokens), :] = upper
        low[pl.ds(n * tokens, tokens), :] = (weights - upper.astype(jnp.float32)).astype(jnp.bfloat16)
    for k in range(0, CHIPS, 2):
        pair = dot(turned[...], chosen[:, k * WIDE : (k + 2) * WIDE]).astype(jnp.bfloat16)
        blocks[k][...] = pair[:, :WIDE]
        blocks[k + 1][...] = pair[:, WIDE:]


def route(own, other):
    top_count, tokens, feat = own[2].shape
    width = CHIPS * WIDE
    outs = [jax.ShapeDtypeStruct((feat, WIDE), jnp.bfloat16)] * CHIPS
    outs += [jax.ShapeDtypeStruct((2 * tokens, width), jnp.bfloat16)] * 2
    got = pl.pallas_call(
        route_kernel,
        out_shape=outs,
        scratch_shapes=[
            pltpu.VMEM((feat, 2 * top_count * tokens), jnp.bfloat16),
            pltpu.VMEM((2 * top_count * tokens, width), jnp.bfloat16),
        ],
        compiler_params=pltpu.CompilerParams(vmem_limit_bytes=VMEM),
        name="route",
    )(*own, *other)
    return got[:CHIPS], got[CHIPS], got[CHIPS + 1]


def ring_kernel(x_first, early, factor, *rest):
    sources, rest = rest[: 3 if early else 2], rest[3 if early else 2 :]
    before, outs, (held, gathered, sems) = rest[:-3][: 1 - early], rest[1 - early : -3], rest[-3:]
    panel = lax.axis_index("panel")
    x, y = panel // SIDE, panel % SIDE
    feat, half = held.shape[1], held.shape[1] // 2
    width = gathered.shape[2]
    copies = []
    for g, second in enumerate(range(SIDE - 1) if early else (SIDE - 1,)):
        for first in range(SIDE):
            dx, dy = (STEPS[first], STEPS[second]) if x_first else (STEPS[second], STEPS[first])
            owner = (x + dx + SIDE) % SIDE * SIDE + (y + dy + SIDE) % SIDE
            lead = owner % 2 * (WINDOW - feat)
            top = first * WINDOW
            gathered[g, pl.ds(top, WINDOW - feat), :] = jnp.zeros((WINDOW - feat, width), gathered.dtype)
            gathered[g, pl.ds(top + feat, WINDOW - feat), :] = jnp.zeros((WINDOW - feat, width), gathered.dtype)
            columns = pl.ds(pl.multiple_of(owner * feat - lead, 128), WINDOW)
            window = held.at[g, :, pl.ds(top, WINDOW)]
            copies.append(pltpu.make_async_copy(factor.at[:, columns], window, sems.at[len(copies)]))
            copies[-1].start()
            for j in range(2):
                source = sources[second].at[j, first] if early else sources[j].at[first]
                target = gathered.at[g, pl.ds(pl.multiple_of(top + j * half + lead, 16), half)]
                copies.append(pltpu.make_async_copy(source, target, sems.at[len(copies)]))
                copies[-1].start()
    count = len(copies) // held.shape[0]
    if early:
        for g in range(held.shape[0]):
            for copy in copies[g * count : (g + 1) * count]:
                copy.wait()
            total = dot(held[g], gathered[g])
            outs[0][...] = total if g == 0 else total + outs[0][...]
        return
    total = before[0][...]
    for first in range(SIDE):
        for copy in copies[first * 3 : first * 3 + 3]:
            copy.wait()
        span = pl.ds(first * WINDOW, WINDOW)
        total += dot(held[0, :, span], gathered[0, span, :])
    total = total.astype(jnp.bfloat16)
    for b, block in enumerate(outs):
        block[...] = total[:, b * WIDE : (b + 1) * WIDE]


def times_ring(factor, x_first, pieces, before=()):
    feat, full = factor.shape
    width = pieces[0].shape[-1]
    early = not before
    groups = SIDE - 1 if early else 1
    anywhere, vmem = pl.BlockSpec(memory_space=pl.ANY), pl.BlockSpec(memory_space=pltpu.VMEM)
    if early:
        outs = [jax.ShapeDtypeStruct((feat, width), jnp.float32)]
    else:
        outs = [jax.ShapeDtypeStruct((feat, WIDE), jnp.bfloat16)] * (width // WIDE)
    depth = SIDE * WINDOW
    return pl.pallas_call(
        functools.partial(ring_kernel, x_first, early),
        in_specs=[anywhere] * (1 + len(pieces)) + [vmem] * len(before),
        out_specs=[vmem] * len(outs),
        out_shape=outs,
        scratch_shapes=[
            pltpu.VMEM((groups, feat, depth), jnp.bfloat16),
            pltpu.VMEM((groups, depth, width), jnp.bfloat16),
            pltpu.SemaphoreType.DMA((groups * SIDE * 3,)),
        ],
        compiler_params=pltpu.CompilerParams(vmem_limit_bytes=VMEM),
        cost_estimate=pl.CostEstimate(
            flops=2 * groups * feat * depth * width,
            bytes_accessed=2 * groups * depth * (feat + width),
            transcendentals=0,
        ),
        name="times_ring_early" if early else "times_ring_late",
    )(factor, *pieces, *before)


def go_round(parts, way):
    behind, ahead = (lax.ppermute(parts, "panel", way(by)) for by in (1, -1))
    return behind, ahead, lax.ppermute(behind[0], "panel", way(1)), lax.ppermute(ahead[1], "panel", way(-1))


def ring_gather(blocks, x_first):
    block = jnp.concatenate(blocks, 1)
    feat, width = block.shape
    ways = (along_x, along_y) if x_first else (along_y, along_x)
    mine = block.reshape(2, feat // 2, width)
    behind, ahead, *across = go_round(mine, ways[0])
    line = jnp.stack([jnp.stack([mine[j], behind[j], ahead[j], across[j]]) for j in range(2)])
    behind, ahead, *across = go_round(line, ways[1])
    return [line, behind, ahead], across


def combine_kernel(count, high, low, *rest):
    returned, (own, other) = rest[:count], rest[count:]
    tokens = own.shape[0]
    total = None
    for k, block in enumerate(returned):
        span = pl.ds(k * WIDE, WIDE)
        for part in (high, low):
            term = dot(part[:, span], block[...], ((1,), (1,)))
            total = term if total is None else total + term
    own[...] = total[:tokens]
    other[...] = total[tokens:]


def combine(high, low, returned):
    feat = returned[0].shape[0]
    return pl.pallas_call(
        functools.partial(combine_kernel, len(returned)),
        out_shape=[jax.ShapeDtypeStruct((high.shape[0] // 2, feat), jnp.float32)] * 2,
        compiler_params=pltpu.CompilerParams(vmem_limit_bytes=VMEM),
        name="combine",
    )(high, low, *returned)


def on_device(queries, expert_ids, mix_weights, factors):
    swap = lambda a: lax.ppermute(a, "expert", SWAP)
    mine = expert_ids.T, mix_weights.T, jnp.transpose(queries, (1, 0, 2))
    blocks, high, low = route(mine, tuple(map(swap, mine)))
    after = lax.optimization_barrier
    send = lambda k, a: lax.ppermute(a, "expert", along_z(k)) if k % CHIPS else a
    first = [send(k, blocks[k]) for k in X_FIRST]
    second = [send(k, blocks[k]) for k in Y_FIRST]

    factor = factors[0]
    near_x, far_x = ring_gather(first, True)
    near_y, far_y = ring_gather(second, False)
    early_x = times_ring(factor, True, near_x)
    early_y = times_ring(factor, False, near_y)
    far_x, early_y = after((far_x, early_y))
    late_x = times_ring(factor, True, far_x, early_x)
    late_y = times_ring(factor, False, far_y, early_y)

    returned = {k: send(-k, block) for k, block in zip(X_FIRST + Y_FIRST, late_x + late_y)}
    returned = [returned[k] for k in range(CHIPS)]
    own, other = combine(high, low, returned)
    return (own + swap(other)).astype(jnp.bfloat16)


def solution(mesh):
    in_specs = (
        P("expert", None, "panel"),
        P("expert", None),
        P("expert", None),
        P("expert", "panel", None),
    )
    out_specs = P("expert", "panel")
    return jax.shard_map(
        on_device, mesh=mesh, in_specs=in_specs, out_specs=out_specs, check_vma=False
    )
```

```python
import functools

import jax
import jax.numpy as jnp
from jax import lax
from jax.experimental import pallas as pl
from jax.experimental.pallas import tpu as pltpu
from jax.sharding import PartitionSpec as P

SIDE = 4
CHIPS = 8
SLOTS = 64
WIDE = 2 * SLOTS
X_FIRST = (2, 6, 3, 5)
Y_FIRST = (0, 1, 7, 4)
WINDOW = 512
STEPS = (0, -1, 1, 2)
VMEM = 50 * 1024 * 1024


def along_x(by):
    return [(x * SIDE + y, (x + by) % SIDE * SIDE + y) for x in range(SIDE) for y in range(SIDE)]


def along_y(by):
    return [(x * SIDE + y, x * SIDE + (y + by) % SIDE) for x in range(SIDE) for y in range(SIDE)]


def along_z(by):
    return [(z * 2 + c, (z + by) % CHIPS * 2 + c) for z in range(CHIPS) for c in range(2)]


SWAP = [(i, i ^ 1) for i in range(2 * CHIPS)]


def dot(a, b, dims=((1,), (0,))):
    return lax.dot_general(a, b, (dims, ((), ())), preferred_element_type=jnp.float32)


def route_kernel(own_ids, own_mix, own_rows, other_ids, other_mix, other_rows, *rest):
    blocks, (high, low), (turned, chosen) = rest[:CHIPS], rest[CHIPS : CHIPS + 2], rest[CHIPS + 2 :]
    me = lax.axis_index("expert")
    z, core = me // 2, me % 2
    top_count, tokens, _ = own_rows.shape
    width = CHIPS * WIDE
    lane = lax.broadcasted_iota(jnp.int32, (tokens, width), 1)
    earlier = (
        lax.broadcasted_iota(jnp.int32, (tokens, tokens), 0)
        > lax.broadcasted_iota(jnp.int32, (tokens, tokens), 1)
    ).astype(jnp.bfloat16)
    experts = lax.broadcasted_iota(jnp.int32, (tokens, 2 * CHIPS), 1)
    sides = (own_ids, own_mix, own_rows), (other_ids, other_mix, other_rows)
    for n, (ids, mix, rows) in enumerate(sides):
        source = core if n == 0 else 1 - core
        ids, mix = ids[...].T, mix[...].T
        named = [ids[:, j : j + 1] for j in range(top_count)]
        hits = [(experts == one).astype(jnp.float32) for one in named]
        before = dot(earlier, sum(hits).astype(jnp.bfloat16))
        weights = jnp.zeros((tokens, width), jnp.float32)
        for j in range(top_count):
            slot = jnp.sum(hits[j] * before, axis=1, keepdims=True).astype(jnp.int32)
            shift = ((named[j] >> 1) - z + CHIPS) & (CHIPS - 1)
            place = jnp.where((named[j] & 1) == core, shift * WIDE + source * SLOTS + slot, -1)
            taken = lane == place
            span = pl.ds((n * top_count + j) * tokens, tokens)
            chosen[span, :] = taken.astype(jnp.float32).astype(jnp.bfloat16)
            turned[:, span] = rows[j].T
            weights = jnp.where(taken, mix[:, j : j + 1], weights)
        upper = weights.astype(jnp.bfloat16)
        high[pl.ds(n * tokens, tokens), :] = upper
        low[pl.ds(n * tokens, tokens), :] = (weights - upper.astype(jnp.float32)).astype(jnp.bfloat16)
    for k in range(0, CHIPS, 2):
        pair = dot(turned[...], chosen[:, k * WIDE : (k + 2) * WIDE]).astype(jnp.bfloat16)
        blocks[k][...] = pair[:, :WIDE]
        blocks[k + 1][...] = pair[:, WIDE:]


def route(own, other):
    top_count, tokens, feat = own[2].shape
    width = CHIPS * WIDE
    outs = [jax.ShapeDtypeStruct((feat, WIDE), jnp.bfloat16)] * CHIPS
    outs += [jax.ShapeDtypeStruct((2 * tokens, width), jnp.bfloat16)] * 2
    got = pl.pallas_call(
        route_kernel,
        out_shape=outs,
        scratch_shapes=[
            pltpu.VMEM((feat, 2 * top_count * tokens), jnp.bfloat16),
            pltpu.VMEM((2 * top_count * tokens, width), jnp.bfloat16),
        ],
        compiler_params=pltpu.CompilerParams(vmem_limit_bytes=VMEM),
        name="route",
    )(*own, *other)
    return got[:CHIPS], got[CHIPS], got[CHIPS + 1]


def ring_kernel(x_first, early, factor, *rest):
    sources, rest = rest[: 3 if early else 2], rest[3 if early else 2 :]
    before, outs, (held, gathered, sems) = rest[:-3][: 1 - early], rest[1 - early : -3], rest[-3:]
    panel = lax.axis_index("panel")
    x, y = panel // SIDE, panel % SIDE
    feat, half = held.shape[1], held.shape[1] // 2
    width = gathered.shape[2]
    copies, blanks = [], []
    for g, second in enumerate(range(SIDE - 1) if early else (SIDE - 1,)):
        for first in range(SIDE):
            dx, dy = (STEPS[first], STEPS[second]) if x_first else (STEPS[second], STEPS[first])
            owner = (x + dx + SIDE) % SIDE * SIDE + (y + dy + SIDE) % SIDE
            lead = owner % 2 * (WINDOW - feat)
            top = first * WINDOW
            blanks.append((g, pl.multiple_of(top + (1 - owner % 2) * feat, 16)))
            columns = pl.ds(pl.multiple_of(owner * feat - lead, 128), WINDOW)
            window = held.at[g, :, pl.ds(top, WINDOW)]
            copies.append(pltpu.make_async_copy(factor.at[:, columns], window, sems.at[len(copies)]))
            copies[-1].start()
            for j in range(2):
                source = sources[second].at[j, first] if early else sources[j].at[first]
                target = gathered.at[g, pl.ds(pl.multiple_of(top + j * half + lead, 16), half)]
                copies.append(pltpu.make_async_copy(source, target, sems.at[len(copies)]))
                copies[-1].start()
    for g, top in blanks:
        gathered[g, pl.ds(top, WINDOW - feat), :] = jnp.zeros((WINDOW - feat, width), gathered.dtype)
    count = len(copies) // held.shape[0]
    if early:
        for g in range(held.shape[0]):
            for copy in copies[g * count : (g + 1) * count]:
                copy.wait()
            total = dot(held[g], gathered[g])
            outs[0][...] = total if g == 0 else total + outs[0][...]
        return
    total = before[0][...]
    for first in range(0, SIDE, 2):
        for copy in copies[first * 3 : first * 3 + 6]:
            copy.wait()
        span = pl.ds(first * WINDOW, 2 * WINDOW)
        total += dot(held[0, :, span], gathered[0, span, :])
    total = total.astype(jnp.bfloat16)
    for b, block in enumerate(outs):
        block[...] = total[:, b * WIDE : (b + 1) * WIDE]


def times_ring(factor, x_first, pieces, before=()):
    feat, full = factor.shape
    width = pieces[0].shape[-1]
    early = not before
    groups = SIDE - 1 if early else 1
    anywhere, vmem = pl.BlockSpec(memory_space=pl.ANY), pl.BlockSpec(memory_space=pltpu.VMEM)
    if early:
        outs = [jax.ShapeDtypeStruct((feat, width), jnp.float32)]
    else:
        outs = [jax.ShapeDtypeStruct((feat, WIDE), jnp.bfloat16)] * (width // WIDE)
    depth = SIDE * WINDOW
    return pl.pallas_call(
        functools.partial(ring_kernel, x_first, early),
        in_specs=[anywhere] * (1 + len(pieces)) + [vmem] * len(before),
        out_specs=[vmem] * len(outs),
        out_shape=outs,
        scratch_shapes=[
            pltpu.VMEM((groups, feat, depth), jnp.bfloat16),
            pltpu.VMEM((groups, depth, width), jnp.bfloat16),
            pltpu.SemaphoreType.DMA((groups * SIDE * 3,)),
        ],
        compiler_params=pltpu.CompilerParams(vmem_limit_bytes=VMEM),
        cost_estimate=pl.CostEstimate(
            flops=2 * groups * feat * depth * width,
            bytes_accessed=2 * groups * depth * (feat + width),
            transcendentals=0,
        ),
        name="times_ring_early" if early else "times_ring_late",
    )(factor, *pieces, *before)


def go_round(parts, way):
    behind, ahead = (lax.ppermute(parts, "panel", way(by)) for by in (1, -1))
    return behind, ahead, lax.ppermute(behind[0], "panel", way(1)), lax.ppermute(ahead[1], "panel", way(-1))


def ring_gather(blocks, x_first):
    block = jnp.concatenate(blocks, 1)
    feat, width = block.shape
    ways = (along_x, along_y) if x_first else (along_y, along_x)
    mine = block.reshape(2, feat // 2, width)
    behind, ahead, *across = go_round(mine, ways[0])
    line = jnp.stack([jnp.stack([mine[j], behind[j], ahead[j], across[j]]) for j in range(2)])
    behind, ahead, *across = go_round(line, ways[1])
    return [line, behind, ahead], across


def combine_kernel(count, high, low, *rest):
    returned, (own, other) = rest[:count], rest[count:]
    tokens = own.shape[0]
    total = None
    for k, block in enumerate(returned):
        span = pl.ds(k * WIDE, WIDE)
        for part in (high, low):
            term = dot(part[:, span], block[...], ((1,), (1,)))
            total = term if total is None else total + term
    own[...] = total[:tokens]
    other[...] = total[tokens:]


def combine(high, low, returned):
    feat = returned[0].shape[0]
    return pl.pallas_call(
        functools.partial(combine_kernel, len(returned)),
        out_shape=[jax.ShapeDtypeStruct((high.shape[0] // 2, feat), jnp.float32)] * 2,
        compiler_params=pltpu.CompilerParams(vmem_limit_bytes=VMEM),
        name="combine",
    )(high, low, *returned)


def on_device(queries, expert_ids, mix_weights, factors):
    swap = lambda a: lax.ppermute(a, "expert", SWAP)
    mine = expert_ids.T, mix_weights.T, jnp.transpose(queries, (1, 0, 2))
    blocks, high, low = route(mine, tuple(map(swap, mine)))
    after = lax.optimization_barrier
    send = lambda k, a: lax.ppermute(a, "expert", along_z(k)) if k % CHIPS else a
    first = [send(k, blocks[k]) for k in X_FIRST]
    second = [send(k, blocks[k]) for k in Y_FIRST]

    factor = factors[0]
    near_x, far_x = ring_gather(first, True)
    near_y, far_y = ring_gather(second, False)
    early_x = times_ring(factor, True, near_x)
    early_y = times_ring(factor, False, near_y)
    far_x, early_y = after((far_x, early_y))
    late_x = times_ring(factor, True, far_x, early_x)
    late_y = times_ring(factor, False, far_y, early_y)

    returned = {k: send(-k, block) for k, block in zip(X_FIRST + Y_FIRST, late_x + late_y)}
    returned = [returned[k] for k in range(CHIPS)]
    own, other = combine(high, low, returned)
    return (own + swap(other)).astype(jnp.bfloat16)


def solution(mesh):
    in_specs = (
        P("expert", None, "panel"),
        P("expert", None),
        P("expert", None),
        P("expert", "panel", None),
    )
    out_specs = P("expert", "panel")
    return jax.shard_map(
        on_device, mesh=mesh, in_specs=in_specs, out_specs=out_specs, check_vma=False
    )
```
